32 devices in a mesh: grp: 2 (over y), vv: 4 (over z), oo: 2 (over core), rep: 2 (over x).
Axes of the slice: x: 2, y: 2, z: 4, core: 2. Of those that a mesh axis runs over, the one named last changes fastest.
Arguments:
- amplitudes: bfloat16 [8192, 4096], P(('grp', 'vv'), ('oo', 'rep')), parts along dimension 0, may hold values from -6 to 6
- integrals: bfloat16 [8, 4096, 16384], P(None, ('oo', 'rep'), ('grp', 'vv')), parts along dimension 2, may hold values from -0.125 to 0.125
- occ_irrep: int32 [64], replicated, may hold values from 0 to 7
- virt_count: int32 [8], replicated, may hold values from 1 to 128, 640 in all
- c_irrep: int32 [32], replicated, may hold values from 0 to 7
- a_irrep: int32 [64], replicated, may hold values from 0 to 7
Outputs:
- ladder: bfloat16 [4096, 16384], P(('oo', 'rep'), ('grp', 'vv')), parts along dimension 1
The draws below stay inside these ranges and needn't reach their ends.
There are 2 independent parts, one for each index of `grp`. The reference program is written for one: setup_inputs(seed, part) draws one part's arguments, and reference() takes and returns one part's arrays. A program takes and returns all parts, laid end to end along the dimension named above; an argument that names none is the same for every part. Nothing has to cross between parts.
Inputs may be any that keep to these rules, and one draw needn't show every extreme that they name: `virt_count`: the counts of the 8 irreps sum to 640; the largest is exactly 128.
All inputs are finite; a program needn't handle non-finite values.
Results may differ from the reference program's by a relative error of at most 0.01.
Values may be sent and summed in bfloat16 or wider, within the bound.
A program may use at most 192 MiB of HBM per device.

```python
import math
import jax
import jax.numpy as jnp
import numpy as np
from jax import lax

O = 64
V = 640
VMAX = 128
C_WIN = 32
A_WIN = 64
PAIRS = 4096
KDIM = 4096
QDIM = 8192
TILE = 256
N_OO = 2
N_REP = 2


def set_ends(result, rng, smallest, high):
    extent = result.shape
    index_at = [jax.random.randint(jax.random.fold_in(rng, axis), (), 0, extent[axis]) for axis in range(len(extent))]
    result = result.at[tuple(index_at)].set(smallest)
    longest = extent.index(max(extent))
    index_at[longest] = (index_at[longest] + 1) % extent[longest]
    return result.at[tuple(index_at)].set(high)


def shard_levels(key, dims, split, low, top_value):
    def one(dim, blocks):
        draws = jax.random.uniform(jax.random.fold_in(jax.random.fold_in(key, 6), dim), (blocks,), jnp.float32, low / len(split), top_value / len(split))
        return jnp.repeat(jnp.exp(draws), dims[dim] // blocks).reshape((-1,) + (1,) * (len(dims) - dim - 1))

    gain = one(*split[0])
    for cut in split[1:]:
        gain = gain * one(*cut)
    return gain


def split_up(number_of, total, reach, skew):
    weights = [(1 << 20) // math.isqrt(grade ** skew) + 1 for grade in range(2, number_of + 1)]
    rest, holding = total - reach - (number_of - 1), [1] * (number_of - 1)
    while rest > 0:
        free = [i for i in range(number_of - 1) if holding[i] < reach]
        whole, budget = sum([weights[i] for i in free]), rest
        for i in free:
            more = min(reach - holding[i], max(1, budget * weights[i] // whole), rest)
            holding[i] = holding[i] + more
            rest = rest - more
    return np.array([reach] + holding)


def uneven(stream_key, count, total, most, skew):
    if count == 2:
        one = jax.random.randint(stream_key, (), max(1, total - most), min(most, total - 1) + 1)
        return jnp.stack([one, total - one])
    sizes = jnp.asarray(split_up(count, total, most, skew), jnp.int32)
    pairs = (count - 1) // 2
    giver, receiver = sizes[1:1 + 2 * pairs:2], sizes[2:2 + 2 * pairs:2]
    slack = jnp.minimum(giver - 1, most - receiver)
    moved = jax.random.randint(jax.random.fold_in(stream_key, 1), (pairs,), 0, 1 << 20) % (slack + 1)
    sizes = sizes.at[1:1 + 2 * pairs:2].set(giver - moved).at[2:2 + 2 * pairs:2].set(receiver + moved)
    return sizes[jax.random.permutation(jax.random.fold_in(stream_key, 2), count)]


def bell_draw(rng, dims, deviation, limit, split=(), kind=jnp.bfloat16):
    level = shard_levels(rng, dims, split, -0.22, 0.18) if split else 1.0
    drawn = jax.random.normal(rng, dims, jnp.float32) * deviation * level
    return jnp.minimum(jnp.maximum(drawn, -limit), limit).astype(kind)


def setup_inputs(seed: int = 0, part: int = 0) -> dict:
    seeds = jax.random.split(jax.random.key(seed), 7)
    own_keys = jax.random.split(jax.random.fold_in(seeds[6], part), 7)
    return {
        "amplitudes": bell_draw(own_keys[0], (PAIRS, KDIM), 1.0, 6.0, ((0, 4), (1, 4))),
        "integrals": bell_draw(own_keys[1], (8, KDIM, QDIM), (KDIM // 2) ** -0.5, 0.125, ((1, 4), (2, 4))),
        "occ_irrep": set_ends(jax.random.randint(seeds[2], (O,), 0, 8), jax.random.fold_in(seeds[2], 1), 0, 7).astype(jnp.int32),
        "virt_count": uneven(seeds[3], 8, V, VMAX, 1).astype(jnp.int32),
        "c_irrep": set_ends(jax.random.randint(seeds[4], (C_WIN,), 0, 8), jax.random.fold_in(seeds[4], 1), 0, 7).astype(jnp.int32),
        "a_irrep": set_ends(jax.random.randint(seeds[5], (A_WIN,), 0, 8), jax.random.fold_in(seeds[5], 1), 0, 7).astype(jnp.int32),
    }


def lookup(labels_in, table_values):
    hits = labels_in[..., None] == jnp.arange(table_values.shape[0], dtype=jnp.int32)
    return jnp.sum(jnp.where(hits, table_values, 0), axis=-1, dtype=jnp.int32)


def slot_valid(slot_index, slot_irrep, virt_count):
    orbital_slot = slot_index // VMAX
    position = slot_index % VMAX
    slot_label = lookup(orbital_slot, slot_irrep)
    irreps_all = jnp.arange(8, dtype=jnp.int32)[:, None]
    needed = jnp.bitwise_xor(irreps_all, slot_label[None, :])
    return position[None, :] < lookup(needed, virt_count)


def pair_irreps(occ_irrep, pair_count):
    pair_ids = jnp.arange(pair_count, dtype=jnp.int32)
    return jnp.bitwise_xor(lookup(pair_ids // O, occ_irrep), lookup(pair_ids % O, occ_irrep))


def tile_layout(row_irrep, tile_rows, tile_total):
    labels_all = jnp.arange(8, dtype=jnp.int32)
    member = (row_irrep[:, None] == labels_all[None, :]).astype(jnp.int32)
    counts = jnp.sum(member, axis=0, dtype=jnp.int32)
    before = jnp.cumsum(member, axis=0, dtype=jnp.int32) - member
    rank_in = jnp.sum(before * member, axis=1, dtype=jnp.int32)
    tile_counts = (counts + tile_rows - 1) // tile_rows
    tile_ends = jnp.cumsum(tile_counts, dtype=jnp.int32)
    tile_starts = tile_ends - tile_counts
    position = jnp.sum(member * tile_starts[None, :], axis=1, dtype=jnp.int32) * tile_rows + rank_in
    slots_total = tile_total * tile_rows
    row_numbers = jnp.arange(row_irrep.shape[0], dtype=jnp.int32)
    source = jnp.zeros((slots_total,), jnp.int32).at[position].set(row_numbers)
    filled = jnp.zeros((slots_total,), jnp.int32).at[position].set(jnp.ones_like(row_numbers))
    tile_ids = jnp.arange(tile_total, dtype=jnp.int32)
    passed = (tile_ends[None, :] <= tile_ids[:, None]).astype(jnp.int32)
    tile_irrep = jnp.minimum(jnp.sum(passed, axis=1, dtype=jnp.int32), 7)
    return position, source, filled, tile_irrep


def ladder_tiles(row_block_all, integrals, k_valid, q_valid, layout, tile_rows, tile_total, pieces):
    position, source, filled, tile_irrep = layout
    zero_value = jnp.zeros((), integrals.dtype)

    def one_tile(state_in, tile_id):
        source_rows = lax.dynamic_slice_in_dim(source, tile_id * tile_rows, tile_rows)
        filled_now = lax.dynamic_slice_in_dim(filled, tile_id * tile_rows, tile_rows)
        row_block = jnp.where(filled_now[:, None] > 0, row_block_all[source_rows], zero_value)
        irrep_now = tile_irrep[tile_id]
        weights = jnp.where(k_valid[irrep_now][:, None] & q_valid[irrep_now][None, :], integrals[irrep_now], zero_value)
        total = jnp.zeros((tile_rows, integrals.shape[2]), jnp.float32)
        for piece_lo, piece_hi in pieces:
            product = jnp.dot(row_block[:, piece_lo:piece_hi], weights[piece_lo:piece_hi], preferred_element_type=jnp.float32)
            total = total + lax.optimization_barrier(product.astype(jnp.bfloat16)).astype(jnp.float32)
        return state_in, total

    _, outputs = lax.scan(one_tile, jnp.int32(0), jnp.arange(tile_total, dtype=jnp.int32))
    flat = outputs.reshape(tile_total * tile_rows, integrals.shape[2])
    return flat[position]


def reference(amplitudes, integrals, occ_irrep, virt_count, c_irrep, a_irrep):
    row_irrep = pair_irreps(occ_irrep, O * O)
    k_valid = slot_valid(jnp.arange(C_WIN * VMAX, dtype=jnp.int32), c_irrep, virt_count)
    q_valid = slot_valid(jnp.arange(A_WIN * VMAX, dtype=jnp.int32), a_irrep, virt_count)
    tile_total = O * O // TILE + 8
    layout = tile_layout(row_irrep, TILE, tile_total)
    piece_width = C_WIN * VMAX // (N_OO * N_REP)
    pieces = [(piece_index * piece_width, (piece_index + 1) * piece_width) for piece_index in range(N_OO * N_REP)]
    ladder = ladder_tiles(amplitudes, integrals, k_valid, q_valid, layout, TILE, tile_total, pieces)
    return ladder.astype(jnp.bfloat16)
```

```python
import functools

import jax
import jax.numpy as jnp
from jax import lax
from jax.experimental import pallas as pl
from jax.experimental.pallas import tpu as pltpu
from jax.sharding import PartitionSpec as P

O = 64
VMAX = 128
TILE = 256


def lookup(labels_in, table_values):
    hits = labels_in[..., None] == jnp.arange(table_values.shape[0], dtype=jnp.int32)
    return jnp.sum(jnp.where(hits, table_values, 0), axis=-1, dtype=jnp.int32)


def slot_valid(slot_index, slot_irrep, virt_count):
    orbital_slot = slot_index // VMAX
    position = slot_index % VMAX
    slot_label = lookup(orbital_slot, slot_irrep)
    irreps_all = jnp.arange(8, dtype=jnp.int32)[:, None]
    needed = jnp.bitwise_xor(irreps_all, slot_label[None, :])
    return position[None, :] < lookup(needed, virt_count)


def pair_irreps(occ_irrep, pair_count):
    pair_ids = jnp.arange(pair_count, dtype=jnp.int32)
    return jnp.bitwise_xor(lookup(pair_ids // O, occ_irrep), lookup(pair_ids % O, occ_irrep))


def tile_layout(row_irrep, tile_rows, tile_total):
    labels_all = jnp.arange(8, dtype=jnp.int32)
    member = (row_irrep[:, None] == labels_all[None, :]).astype(jnp.int32)
    counts = jnp.sum(member, axis=0, dtype=jnp.int32)
    before = jnp.cumsum(member, axis=0, dtype=jnp.int32) - member
    rank_in = jnp.sum(before * member, axis=1, dtype=jnp.int32)
    tile_counts = (counts + tile_rows - 1) // tile_rows
    tile_ends = jnp.cumsum(tile_counts, dtype=jnp.int32)
    tile_starts = tile_ends - tile_counts
    position = jnp.sum(member * tile_starts[None, :], axis=1, dtype=jnp.int32) * tile_rows + rank_in
    slots_total = tile_total * tile_rows
    row_numbers = jnp.arange(row_irrep.shape[0], dtype=jnp.int32)
    source = jnp.zeros((slots_total,), jnp.int32).at[position].set(row_numbers)
    filled = jnp.zeros((slots_total,), jnp.int32).at[position].set(jnp.ones_like(row_numbers))
    tile_ids = jnp.arange(tile_total, dtype=jnp.int32)
    passed = (tile_ends[None, :] <= tile_ids[:, None]).astype(jnp.int32)
    tile_irrep = jnp.minimum(jnp.sum(passed, axis=1, dtype=jnp.int32), 7)
    return (position, source, filled, tile_irrep)


def ladder_tiles(row_block_all, integrals, k_valid, q_valid, layout, tile_rows, tile_total):
    position, source, filled, tile_irrep = layout
    zero_value = jnp.zeros((), integrals.dtype)

    def one_tile(state_in, tile_id):
        source_rows = lax.dynamic_slice_in_dim(source, tile_id * tile_rows, tile_rows)
        filled_now = lax.dynamic_slice_in_dim(filled, tile_id * tile_rows, tile_rows)
        row_block = jnp.where(filled_now[:, None] > 0, row_block_all[source_rows], zero_value)
        irrep_now = tile_irrep[tile_id]
        weights = jnp.where(
            k_valid[irrep_now][:, None] & q_valid[irrep_now][None, :],
            integrals[irrep_now],
            zero_value,
        )
        product = jnp.dot(row_block, weights, preferred_element_type=jnp.float32)
        return (
            state_in,
            lax.optimization_barrier(product.astype(jnp.bfloat16)).astype(jnp.float32),
        )

    _, outputs = lax.scan(one_tile, jnp.int32(0), jnp.arange(tile_total, dtype=jnp.int32))
    flat = outputs.reshape(tile_total * tile_rows, integrals.shape[2])
    return flat[position]


def local(amplitudes, integrals, occ_irrep, virt_count, c_irrep, a_irrep):
    n_rep = lax.axis_size("rep")
    k_local = amplitudes.shape[1]
    q_local = integrals.shape[2]
    pair_total = amplitudes.shape[0] * lax.axis_size("vv")
    k_first = (lax.axis_index("oo") * n_rep + lax.axis_index("rep")) * k_local
    q_first = lax.axis_index("vv") * q_local
    k_valid = slot_valid(k_first + jnp.arange(k_local, dtype=jnp.int32), c_irrep, virt_count)
    q_valid = slot_valid(q_first + jnp.arange(q_local, dtype=jnp.int32), a_irrep, virt_count)
    row_irrep = pair_irreps(occ_irrep, pair_total)
    tile_total = pair_total // TILE + 8
    layout = tile_layout(row_irrep, TILE, tile_total)
    all_rows = lax.all_gather(amplitudes, "vv", axis=0, tiled=True)
    ladder_term = ladder_tiles(all_rows, integrals, k_valid, q_valid, layout, TILE, tile_total)
    summed = lax.psum_scatter(
        ladder_term.astype(jnp.bfloat16), ("oo", "rep"), scatter_dimension=0, tiled=True
    )
    return summed


SUB = 512
T = 128
NT = SUB // T
NP = NT + 7
NH = 8
QC = 512
STRIDE = 64
MESH = pl.DeviceIdType.MESH


def place(step, zz, side):
    middle = ((step + 2) // 4) % 2
    blk_mid = middle * 2 * (step % 2) + (1 - middle) * (1 + 2 * (step // 4))
    half_mid = middle * (step // 2 - 1) + (1 - middle) * (step % 2)
    near = zz * blk_mid + (1 - zz) * (step // 2)
    half = zz * half_mid + (1 - zz) * (step % 2)
    blk = near + side * (3 - 2 * near)
    return near, blk, half


def ladder_kernel(
    tab, src_ref, pos_ref, seg_ref, kval_ref, qval_ref, a_hbm, v_hbm, out_hbm,
    v_all, a_all, a_now, unsort, pairs, tiles, part, core_in, rep_in,
    v_sem, a_sem, z_recv, own_send, fwd_send, core_send, core_recv, rep_send, rep_recv, out_sem,
):
    z = lax.axis_index("vv")
    core = lax.axis_index("oo")
    rep = lax.axis_index("rep")
    side = z // 2
    zz = z + side * (3 - 2 * z)
    outer = (1 - side) * (z - 1) + side * (z + 1)
    inner = (1 - side) * (z + 1) + side * (z - 1)

    def z_copy(h, target, send):
        return pltpu.make_async_remote_copy(
            src_ref=a_all.at[h], dst_ref=a_all.at[h], send_sem=send, recv_sem=z_recv.at[h],
            device_id={"vv": target}, device_id_type=MESH,
        )

    def core_copy(step):
        _, blk, half = place(step, zz, side)
        slot = (blk % 2) * 2 + half
        return pltpu.make_async_remote_copy(
            src_ref=part.at[step % 2], dst_ref=core_in.at[slot],
            send_sem=core_send.at[step % 2], recv_sem=core_recv.at[slot],
            device_id={"oo": 1 - core}, device_id_type=MESH,
        )

    def rep_copy(slot, half):
        return pltpu.make_async_remote_copy(
            src_ref=core_in.at[slot], dst_ref=rep_in.at[half],
            send_sem=rep_send.at[half], recv_sem=rep_recv.at[half],
            device_id={"rep": 1 - rep}, device_id_type=MESH,
        )

    a_copies = [
        pltpu.make_async_copy(a_hbm.at[pl.ds(k * SUB, SUB)], part.at[k, :, pl.ds(0, a_hbm.shape[1])], a_sem.at[k])
        for k in range(2)
    ]
    for copy in a_copies:
        copy.start()
    v_copies = [
        pltpu.make_async_copy(v_hbm.at[r, :, pl.ds(c * QC, QC)], v_all.at[r, c], v_sem.at[r, c])
        for c in range(v_all.shape[1])
        for r in range(8)
    ]
    for copy in v_copies:
        copy.start()

    barrier = pltpu.get_barrier_semaphore()
    pl.semaphore_signal(barrier, inc=1, device_id={"vv": inner}, device_id_type=MESH)
    pl.semaphore_signal(barrier, inc=1, device_id={"oo": 1 - core}, device_id_type=MESH)
    pl.semaphore_signal(barrier, inc=1, device_id={"rep": 1 - rep}, device_id_type=MESH)

    @pl.when(zz == 1)
    def _():
        pl.semaphore_signal(barrier, inc=1, device_id={"vv": outer}, device_id_type=MESH)

    pl.semaphore_wait(barrier, 3 + zz)

    pairs[0] = jnp.zeros_like(pairs[0])
    for k in range(2):
        a_copies[k].wait()
        h = z * 2 + k
        rows = lax.broadcasted_iota(jnp.int32, (SUB, SUB), 0)
        order = (rows == pos_ref[h]).astype(jnp.float32).astype(jnp.bfloat16)
        lanes = lax.broadcasted_iota(jnp.int32, (SUB, 128), 0)
        segs = seg_ref[h]
        label = ((lanes >= segs[0:1]) & (lanes < segs[1:2])).astype(jnp.float32).astype(jnp.bfloat16)
        keep = jnp.dot(label, kval_ref[...], preferred_element_type=jnp.float32)
        moved = jnp.dot(order, part[k, :, 0:a_hbm.shape[1]], preferred_element_type=jnp.float32)
        a_all[h] = (moved * keep).astype(jnp.bfloat16)
        z_copy(h, inner, own_send.at[k]).start()

        @pl.when(zz == 1)
        def _():
            z_copy(h, outer, own_send.at[2 + k]).start()

    for copy in v_copies:
        copy.wait()

    def compute(h, slot):
        for t in range(NT):
            a_now[t] = a_all[h, t * T:(t + 1) * T, :]
        rows = lax.broadcasted_iota(jnp.int32, (SUB, SUB), 0)
        unsort[...] = (rows == src_ref[h]).astype(jnp.float32).astype(jnp.bfloat16)

        def columns(chunk, carry):
            q0 = pl.multiple_of(chunk * QC, QC)

            def pair(p, carry):
                base = h * STRIDE + p * 4
                tile = tab[base]
                irrep = tab[base + 1]
                left = a_now[tile]
                product = jnp.dot(left, v_all[irrep, chunk], preferred_element_type=jnp.float32)
                product = jnp.where(qval_ref[irrep, chunk] > 0, product, 0.0)
                place_in = lax.broadcasted_iota(jnp.int32, (T, QC), 0) + tile * T
                mine = (place_in >= tab[base + 2]) & (place_in < tab[base + 3])
                merged = jnp.where(mine, product, pairs[p].astype(jnp.float32))
                pairs[p + 1] = merged.astype(jnp.bfloat16)
                return carry

            lax.fori_loop(0, NP, pair, 0)
            for t in range(NT):
                tiles[t * T:(t + 1) * T, :] = pairs[tab[h * STRIDE + 48 + t] + 1]
            back = jnp.dot(unsort[...], tiles[...], preferred_element_type=jnp.float32)
            part[slot, :, pl.ds(q0, QC)] = back.astype(jnp.bfloat16)
            return carry

        lax.fori_loop(0, v_all.shape[1], columns, 0)

    def finish(step):
        _, blk, half = place(step, zz, side)
        slot = (blk % 2) * 2 + half

        @pl.when(blk // 2 == core)
        def _():
            core_copy(step).wait_recv()

            def add(c, carry):
                at = pl.ds(pl.multiple_of(c * 64, 64), 64)
                total = core_in[slot, at, :].astype(jnp.float32) + part[step % 2, at, :].astype(jnp.float32)
                core_in[slot, at, :] = total.astype(jnp.bfloat16)
                return carry

            lax.fori_loop(0, SUB // 64, add, 0)

            @pl.when(blk % 2 != rep)
            def _():
                rep_copy(slot, half).start()

    def body(step, carry):
        near, blk, half = place(step, zz, side)
        h = blk * 2 + half

        @pl.when(near != zz)
        def _():
            z_copy(h, inner, own_send.at[0]).wait_recv()

        @pl.when((zz == 1) & (near == 0))
        def _():
            z_copy(h, inner, fwd_send.at[h]).start()

        @pl.when((zz == 1) & (near > 1))
        def _():
            z_copy(h, outer, fwd_send.at[h]).start()

        @pl.when(step >= 2)
        def _():
            _, before, _ = place(step - 2, zz, side)

            @pl.when(before // 2 != core)
            def _():
                core_copy(step - 2).wait_send()

        compute(h, step % 2)

        @pl.when(blk // 2 != core)
        def _():
            core_copy(step).start()

        @pl.when(step >= 1)
        def _():
            finish(step - 1)

        return carry

    lax.fori_loop(0, NH, body, 0)
    finish(NH - 1)

    for step in (NH - 2, NH - 1):
        _, blk, _ = place(step, zz, side)

        @pl.when(blk // 2 != core)
        def _():
            core_copy(step).wait_send()

    outs = []
    for half in range(2):
        rep_copy(rep * 2 + half, half).wait_recv()

        def add(c, carry):
            at = pl.ds(pl.multiple_of(c * 64, 64), 64)
            total = core_in[rep * 2 + half, at, :].astype(jnp.float32) + rep_in[half, at, :].astype(jnp.float32)
            rep_in[half, at, :] = total.astype(jnp.bfloat16)
            return carry

        lax.fori_loop(0, SUB // 64, add, 0)
        copy = pltpu.make_async_copy(rep_in.at[half], out_hbm.at[pl.ds(half * SUB, SUB)], out_sem.at[half])
        copy.start()
        outs.append(copy)
    for half in range(2):
        rep_copy((1 - rep) * 2 + half, half).wait_send()
        z_copy(z * 2 + half, inner, own_send.at[half]).wait_send()

    @pl.when(zz == 1)
    def _():
        for half in range(2):
            z_copy(z * 2 + half, outer, own_send.at[2 + half]).wait_send()
            for near in (0, 2, 3):
                h = (near + side * (3 - 2 * near)) * 2 + half
                z_copy(h, outer, fwd_send.at[h]).wait_send()

    for copy in outs:
        copy.wait()


def exclusive(values, axis):
    return jnp.cumsum(values, axis=axis, dtype=jnp.int32) - values


def layout_tables(row_irrep):
    labels = row_irrep.reshape(NH, 1, SUB)
    member = (labels == jnp.arange(8, dtype=jnp.int32)[None, :, None])
    upper = jnp.arange(SUB)[:, None] < jnp.arange(SUB)[None, :]
    before = jnp.einsum(
        "hrn,nm->hrm", member.astype(jnp.bfloat16), upper.astype(jnp.bfloat16), preferred_element_type=jnp.float32
    ).astype(jnp.int32)
    counts = jnp.sum(member, axis=2, dtype=jnp.int32)
    r8 = jnp.arange(8)
    ends = jnp.sum(jnp.where(r8[None, :, None] >= r8[None, None, :], counts[:, None, :], 0), axis=2, dtype=jnp.int32)
    starts = ends - counts
    pos = jnp.sum(jnp.where(member, before + starts[:, :, None], 0), axis=1, dtype=jnp.int32)
    seats = jnp.arange(SUB, dtype=jnp.int32)
    src = jnp.sum(
        jnp.where(pos[:, None, :] == seats[None, :, None], seats[None, None, :], 0), axis=2, dtype=jnp.int32
    )
    cut = jnp.minimum(ends[:, :7] // T, NT - 1)
    turn = jnp.arange(7, dtype=jnp.int32)[None, :] + cut
    steps = jnp.arange(NP, dtype=jnp.int32)
    irrep = jnp.sum((turn[:, None, :] < steps[None, :, None]).astype(jnp.int32), axis=2, dtype=jnp.int32)
    tile = steps[None, :] - irrep
    pick = irrep[:, :, None] == r8[None, None, :]
    first = jnp.sum(jnp.where(pick, starts[:, None, :], 0), axis=2, dtype=jnp.int32)
    last = jnp.sum(jnp.where(pick, ends[:, None, :], 0), axis=2, dtype=jnp.int32)
    t4 = jnp.arange(NT, dtype=jnp.int32)
    done = t4[None, :] + jnp.sum((cut[:, None, :] <= t4[None, :, None]).astype(jnp.int32), axis=2, dtype=jnp.int32)
    done = jnp.where(t4[None, :] == NT - 1, NP - 1, done)
    rows = jnp.stack([tile, irrep, first, last], axis=2).reshape(NH, NP * 4)
    tab = jnp.concatenate(
        [rows, jnp.zeros((NH, 48 - NP * 4), jnp.int32), done, jnp.zeros((NH, STRIDE - 48 - NT), jnp.int32)], axis=1
    ).reshape(NH * STRIDE)
    seg = jnp.zeros((NH, 2, 128), jnp.int32).at[:, 0, :8].set(starts).at[:, 1, :8].set(ends)
    return tab, src.reshape(NH, 1, SUB), pos.reshape(NH, 1, SUB), seg


def fused(amplitudes, integrals, occ_irrep, virt_count, c_irrep, a_irrep):
    k_local = amplitudes.shape[1]
    q_local = integrals.shape[2]
    k_first = (lax.axis_index("oo") * lax.axis_size("rep") + lax.axis_index("rep")) * k_local
    q_first = lax.axis_index("vv") * q_local
    k_valid = slot_valid(k_first + jnp.arange(k_local, dtype=jnp.int32), c_irrep, virt_count)
    q_valid = slot_valid(q_first + jnp.arange(q_local, dtype=jnp.int32), a_irrep, virt_count)
    row_irrep = jnp.bitwise_xor(occ_irrep[:, None], occ_irrep[None, :]).reshape(-1)
    tab, src, pos, seg = layout_tables(row_irrep)
    kval = jnp.pad(k_valid.astype(jnp.bfloat16), ((0, 120), (0, 0)))
    qval = q_valid.astype(jnp.float32).reshape(8, q_local // QC, 1, QC)
    vmem = pl.BlockSpec(memory_space=pltpu.VMEM)
    hbm = pl.BlockSpec(memory_space=pl.ANY)
    dma = pltpu.SemaphoreType.DMA
    bf16 = jnp.bfloat16
    return pl.pallas_call(
        ladder_kernel,
        out_shape=jax.ShapeDtypeStruct((2 * SUB, q_local), bf16),
        in_specs=[pl.BlockSpec(memory_space=pltpu.SMEM)] + [vmem] * 5 + [hbm] * 2,
        out_specs=hbm,
        scratch_shapes=[
            pltpu.VMEM((8, q_local // QC, k_local, QC), bf16),
            pltpu.VMEM((NH, SUB, k_local), bf16),
            pltpu.VMEM((NT, T, k_local), bf16),
            pltpu.VMEM((SUB, SUB), bf16),
            pltpu.VMEM((NP + 1, T, QC), bf16),
            pltpu.VMEM((SUB, QC), bf16),
            pltpu.VMEM((2, SUB, q_local), bf16),
            pltpu.VMEM((4, SUB, q_local), bf16),
            pltpu.VMEM((2, SUB, q_local), bf16),
            dma((8, q_local // QC)), dma((2,)), dma((NH,)), dma((4,)), dma((NH,)),
            dma((2,)), dma((4,)), dma((2,)), dma((2,)), dma((2,)),
        ],
        compiler_params=pltpu.CompilerParams(
            collective_id=0, has_side_effects=True, vmem_limit_bytes=64 * 1024 * 1024 - 256 * 1024
        ),
        cost_estimate=pl.CostEstimate(
            flops=2 * NH * NP * T * k_local * q_local, bytes_accessed=40 * 1024 * 1024, transcendentals=0
        ),
    )(tab, src, pos, seg, kval, qval, amplitudes, integrals)


def solution(mesh):
    placed = (
        P(("grp", "vv"), ("oo", "rep")),
        P(None, ("oo", "rep"), ("grp", "vv")),
        P(),
        P(),
        P(),
        P(),
    )
    shape = dict(mesh.shape)
    same = (shape['vv'], shape['oo'], shape['rep'], shape['grp']) == (4, 2, 2, 2)
    return jax.shard_map(
        fused if same else local,
        mesh=mesh,
        in_specs=placed,
        out_specs=P(("oo", "rep"), ("grp", "vv")),
        check_vma=False,
    )
```

```python
import functools

import jax
import jax.numpy as jnp
from jax import lax
from jax.experimental import pallas as pl
from jax.experimental.pallas import tpu as pltpu
from jax.sharding import PartitionSpec as P

O = 64
VMAX = 128
TILE = 256


def lookup(labels_in, table_values):
    hits = labels_in[..., None] == jnp.arange(table_values.shape[0], dtype=jnp.int32)
    return jnp.sum(jnp.where(hits, table_values, 0), axis=-1, dtype=jnp.int32)


def slot_valid(slot_index, slot_irrep, virt_count):
    orbital_slot = slot_index // VMAX
    position = slot_index % VMAX
    slot_label = lookup(orbital_slot, slot_irrep)
    irreps_all = jnp.arange(8, dtype=jnp.int32)[:, None]
    needed = jnp.bitwise_xor(irreps_all, slot_label[None, :])
    return position[None, :] < lookup(needed, virt_count)


def pair_irreps(occ_irrep, pair_count):
    pair_ids = jnp.arange(pair_count, dtype=jnp.int32)
    return jnp.bitwise_xor(lookup(pair_ids // O, occ_irrep), lookup(pair_ids % O, occ_irrep))


def tile_layout(row_irrep, tile_rows, tile_total):
    labels_all = jnp.arange(8, dtype=jnp.int32)
    member = (row_irrep[:, None] == labels_all[None, :]).astype(jnp.int32)
    counts = jnp.sum(member, axis=0, dtype=jnp.int32)
    before = jnp.cumsum(member, axis=0, dtype=jnp.int32) - member
    rank_in = jnp.sum(before * member, axis=1, dtype=jnp.int32)
    tile_counts = (counts + tile_rows - 1) // tile_rows
    tile_ends = jnp.cumsum(tile_counts, dtype=jnp.int32)
    tile_starts = tile_ends - tile_counts
    position = jnp.sum(member * tile_starts[None, :], axis=1, dtype=jnp.int32) * tile_rows + rank_in
    slots_total = tile_total * tile_rows
    row_numbers = jnp.arange(row_irrep.shape[0], dtype=jnp.int32)
    source = jnp.zeros((slots_total,), jnp.int32).at[position].set(row_numbers)
    filled = jnp.zeros((slots_total,), jnp.int32).at[position].set(jnp.ones_like(row_numbers))
    tile_ids = jnp.arange(tile_total, dtype=jnp.int32)
    passed = (tile_ends[None, :] <= tile_ids[:, None]).astype(jnp.int32)
    tile_irrep = jnp.minimum(jnp.sum(passed, axis=1, dtype=jnp.int32), 7)
    return (position, source, filled, tile_irrep)


def ladder_tiles(row_block_all, integrals, k_valid, q_valid, layout, tile_rows, tile_total):
    position, source, filled, tile_irrep = layout
    zero_value = jnp.zeros((), integrals.dtype)

    def one_tile(state_in, tile_id):
        source_rows = lax.dynamic_slice_in_dim(source, tile_id * tile_rows, tile_rows)
        filled_now = lax.dynamic_slice_in_dim(filled, tile_id * tile_rows, tile_rows)
        row_block = jnp.where(filled_now[:, None] > 0, row_block_all[source_rows], zero_value)
        irrep_now = tile_irrep[tile_id]
        weights = jnp.where(
            k_valid[irrep_now][:, None] & q_valid[irrep_now][None, :],
            integrals[irrep_now],
            zero_value,
        )
        product = jnp.dot(row_block, weights, preferred_element_type=jnp.float32)
        return (
            state_in,
            lax.optimization_barrier(product.astype(jnp.bfloat16)).astype(jnp.float32),
        )

    _, outputs = lax.scan(one_tile, jnp.int32(0), jnp.arange(tile_total, dtype=jnp.int32))
    flat = outputs.reshape(tile_total * tile_rows, integrals.shape[2])
    return flat[position]


def local(amplitudes, integrals, occ_irrep, virt_count, c_irrep, a_irrep):
    n_rep = lax.axis_size("rep")
    k_local = amplitudes.shape[1]
    q_local = integrals.shape[2]
    pair_total = amplitudes.shape[0] * lax.axis_size("vv")
    k_first = (lax.axis_index("oo") * n_rep + lax.axis_index("rep")) * k_local
    q_first = lax.axis_index("vv") * q_local
    k_valid = slot_valid(k_first + jnp.arange(k_local, dtype=jnp.int32), c_irrep, virt_count)
    q_valid = slot_valid(q_first + jnp.arange(q_local, dtype=jnp.int32), a_irrep, virt_count)
    row_irrep = pair_irreps(occ_irrep, pair_total)
    tile_total = pair_total // TILE + 8
    layout = tile_layout(row_irrep, TILE, tile_total)
    all_rows = lax.all_gather(amplitudes, "vv", axis=0, tiled=True)
    ladder_term = ladder_tiles(all_rows, integrals, k_valid, q_valid, layout, TILE, tile_total)
    summed = lax.psum_scatter(
        ladder_term.astype(jnp.bfloat16), ("oo", "rep"), scatter_dimension=0, tiled=True
    )
    return summed


SUB = 1024
HALF = 512
T = 256
NT = SUB // T
NP = NT + 7
NH = 4
QC = 512
NQ = 4
STRIDE = 64
MESH = pl.DeviceIdType.MESH


def place(step, zz, side, swap):
    turn = step // 4
    late = turn // 2
    near = late * (turn + swap * (5 - 2 * turn)) + (1 - late) * (turn + zz * (1 - 2 * turn))
    return near, near + side * (3 - 2 * near), step % 4


def ladder_kernel(
    tab, src_ref, pos_ref, seg_ref, kval_ref, qval_ref, a_hbm, v_hbm, out_hbm,
    v_all, a_all, a_now, pairs, tiles, part, core_in, rep_in,
    v_sem, a_sem, z_recv, z_send, core_send, core_recv, rep_send, rep_recv, out_sem,
):
    z = lax.axis_index("vv")
    core = lax.axis_index("oo")
    rep = lax.axis_index("rep")
    side = z // 2
    zz = z + side * (3 - 2 * z)
    outer = (1 - side) * (z - 1) + side * (z + 1)
    inner = (1 - side) * (z + 1) + side * (z - 1)
    swap = 1 - rep - side + 2 * rep * side

    def z_copy(near, half, target, send):
        blk = near + side * (3 - 2 * near)
        at = a_all.at[blk, pl.ds(half * HALF, HALF)]
        return pltpu.make_async_remote_copy(
            src_ref=at, dst_ref=at, send_sem=z_send.at[send], recv_sem=z_recv.at[blk, half],
            device_id={"vv": target}, device_id_type=MESH,
        )

    def arrive(near, half):
        z_copy(near, half, inner, 0).wait_recv()

    sends = [(1, 0, inner, 0), (1, 1, inner, 1), (0, 0, inner, 2), (0, 1, inner, 3), (1, 0, outer, 4), (1, 1, outer, 5)]
    sends += [(2, 0, outer, 6), (2, 1, outer, 7), (3, 0, outer, 8), (3, 1, outer, 9)]

    def send(k):
        z_copy(*sends[k]).start()

    def core_copy(step):
        _, blk, qc = place(step, zz, side, swap)
        slot = (blk % 2) * NQ + qc
        return pltpu.make_async_remote_copy(
            src_ref=part.at[step % 2], dst_ref=core_in.at[slot],
            send_sem=core_send.at[step % 2], recv_sem=core_recv.at[slot],
            device_id={"oo": 1 - core}, device_id_type=MESH,
        )

    def rep_copy(slot, qc):
        return pltpu.make_async_remote_copy(
            src_ref=core_in.at[slot], dst_ref=rep_in.at[qc],
            send_sem=rep_send.at[qc], recv_sem=rep_recv.at[qc],
            device_id={"rep": 1 - rep}, device_id_type=MESH,
        )

    a_copies = [
        pltpu.make_async_copy(a_hbm.at[pl.ds(t * T, T)], a_now.at[t], a_sem.at[t]) for t in range(NT)
    ]
    for copy in a_copies:
        copy.start()
    v_copies = [
        pltpu.make_async_copy(v_hbm.at[r, :, pl.ds(c * QC, QC)], v_all.at[r, c], v_sem.at[r, c])
        for c in range(NQ)
        for r in range(8)
    ]
    for copy in v_copies:
        copy.start()

    barrier = pltpu.get_barrier_semaphore()
    pl.semaphore_signal(barrier, inc=1, device_id={"vv": inner}, device_id_type=MESH)
    pl.semaphore_signal(barrier, inc=1, device_id={"oo": 1 - core}, device_id_type=MESH)
    pl.semaphore_signal(barrier, inc=1, device_id={"rep": 1 - rep}, device_id_type=MESH)

    @pl.when(zz == 1)
    def _():
        pl.semaphore_signal(barrier, inc=1, device_id={"vv": outer}, device_id_type=MESH)

    pl.semaphore_wait(barrier, 3 + zz)

    pairs[0] = jnp.zeros_like(pairs[0])
    for copy in a_copies:
        copy.wait()
    segs = seg_ref[z]
    for t in range(NT):
        rows = lax.broadcasted_iota(jnp.int32, (T, SUB), 0) + t * T
        order = (rows == pos_ref[z]).astype(jnp.float32).astype(jnp.bfloat16)
        lanes = lax.broadcasted_iota(jnp.int32, (T, 128), 0) + t * T
        label = ((lanes >= segs[0:1]) & (lanes < segs[1:2])).astype(jnp.float32).astype(jnp.bfloat16)
        keep = jnp.dot(label, kval_ref[...], preferred_element_type=jnp.float32)
        raw = a_now[...].reshape(SUB, a_now.shape[2])
        moved = jnp.dot(order, raw, preferred_element_type=jnp.float32)
        a_all[z, t * T:(t + 1) * T, :] = (moved * keep).astype(jnp.bfloat16)
        if t % 2 == 1:
            half = t // 2

            @pl.when(zz == 0)
            def _():
                z_copy(0, half, inner, half).start()

            @pl.when(zz == 1)
            def _():
                send(4 + half)

            if half == 0:

                @pl.when(zz == 1)
                def _():
                    send(0)

            else:

                @pl.when((zz == 1) & (swap == 1))
                def _():
                    send(1)

    def load(blk):
        for t in range(NT):
            a_now[t] = a_all[blk, t * T:(t + 1) * T, :]

    def compute(blk, chunk, slot):
        def pair(p, carry):
            base = blk * STRIDE + p * 4
            tile = tab[base]
            irrep = tab[base + 1]
            product = jnp.dot(a_now[tile], v_all[irrep, chunk], preferred_element_type=jnp.float32)
            product = jnp.where(qval_ref[irrep, chunk] > 0, product, 0.0)
            place_in = lax.broadcasted_iota(jnp.int32, (T, QC), 0) + tile * T
            mine = (place_in >= tab[base + 2]) & (place_in < tab[base + 3])
            merged = jnp.where(mine, product, pairs[p].astype(jnp.float32))
            pairs[p + 1] = merged.astype(jnp.bfloat16)
            return carry

        lax.fori_loop(0, NP, pair, 0)
        for t in range(NT):
            tiles[t * T:(t + 1) * T, :] = pairs[tab[blk * STRIDE + 48 + t] + 1]
        for t in range(NT):
            rows = lax.broadcasted_iota(jnp.int32, (T, SUB), 0) + t * T
            unsort = (rows == src_ref[blk]).astype(jnp.float32).astype(jnp.bfloat16)
            back = jnp.dot(unsort, tiles[...], preferred_element_type=jnp.float32)
            part[slot, t * T:(t + 1) * T, :] = back.astype(jnp.bfloat16)

    def finish(step):
        _, blk, qc = place(step, zz, side, swap)
        slot = (blk % 2) * NQ + qc

        @pl.when(blk // 2 == core)
        def _():
            core_copy(step).wait_recv()

            def add(c, carry):
                at = pl.ds(pl.multiple_of(c * 128, 128), 128)
                total = core_in[slot, at, :].astype(jnp.float32) + part[step % 2, at, :].astype(jnp.float32)
                core_in[slot, at, :] = total.astype(jnp.bfloat16)
                return carry

            lax.fori_loop(0, SUB // 128, add, 0)

            @pl.when(blk % 2 != rep)
            def _():
                rep_copy(slot, qc).start()

    def arrivals(step):
        @pl.when((zz == 0) & (step % 4 == 0) & (step > 0))
        def _():
            near, _, _ = place(step, zz, side, swap)
            arrive(near, 0)
            arrive(near, 1)

        @pl.when((zz == 1) & (step == 4))
        def _():
            arrive(0, 0)
            send(2)
            arrive(2, 0)

            @pl.when(swap == 0)
            def _():
                send(6)

            arrive(0, 1)
            send(3)

            @pl.when(swap == 0)
            def _():
                send(1)
                arrive(3 - 1, 1)
                send(7)

            @pl.when(swap == 1)
            def _():
                arrive(3, 0)
                send(8)

        @pl.when((zz == 1) & (swap == 1) & (step == 8))
        def _():
            arrive(3, 1)
            send(9)

        @pl.when((zz == 1) & (swap == 1) & (step == 11))
        def _():
            send(6)

        @pl.when((zz == 1) & (swap == 1) & (step == 12))
        def _():
            arrive(2, 1)
            send(7)

        @pl.when((zz == 1) & (swap == 0) & (step == 10))
        def _():
            arrive(3, 0)
            send(8)

        @pl.when((zz == 1) & (swap == 0) & (step == 12))
        def _():
            arrive(3, 1)
            send(9)

    def body(step, carry):
        _, blk, qc = place(step, zz, side, swap)
        arrivals(step)

        @pl.when(step == 0)
        def _():
            for copy in v_copies:
                copy.wait()

        @pl.when(step >= 2)
        def _():
            _, before, _ = place(step - 2, zz, side, swap)

            @pl.when(before // 2 != core)
            def _():
                core_copy(step - 2).wait_send()

        @pl.when(qc == 0)
        def _():
            load(blk)

        compute(blk, qc, step % 2)

        @pl.when(blk // 2 != core)
        def _():
            core_copy(step).start()

        @pl.when(step >= 1)
        def _():
            finish(step - 1)

        return carry

    lax.fori_loop(0, NH * NQ, body, 0)
    finish(NH * NQ - 1)

    for step in (NH * NQ - 2, NH * NQ - 1):
        _, blk, _ = place(step, zz, side, swap)

        @pl.when(blk // 2 != core)
        def _():
            core_copy(step).wait_send()

    outs = []
    for qc in range(NQ):
        rep_copy(rep * NQ + qc, qc).wait_recv()

        def add(c, carry):
            at = pl.ds(pl.multiple_of(c * 128, 128), 128)
            total = core_in[rep * NQ + qc, at, :].astype(jnp.float32) + rep_in[qc, at, :].astype(jnp.float32)
            rep_in[qc, at, :] = total.astype(jnp.bfloat16)
            return carry

        lax.fori_loop(0, SUB // 128, add, 0)
        copy = pltpu.make_async_copy(rep_in.at[qc], out_hbm.at[:, pl.ds(qc * QC, QC)], out_sem.at[qc])
        copy.start()
        outs.append(copy)
    for qc in range(NQ):
        rep_copy((1 - rep) * NQ + qc, qc).wait_send()

    @pl.when(zz == 0)
    def _():
        for half in range(2):
            z_copy(0, half, inner, half).wait_send()

    @pl.when(zz == 1)
    def _():
        for k in range(10):
            z_copy(*sends[k]).wait_send()

    for copy in outs:
        copy.wait()


def exclusive(values, axis):
    return jnp.cumsum(values, axis=axis, dtype=jnp.int32) - values


def layout_tables(row_irrep):
    labels = row_irrep.reshape(NH, 1, SUB)
    member = (labels == jnp.arange(8, dtype=jnp.int32)[None, :, None])
    upper = jnp.arange(SUB)[:, None] < jnp.arange(SUB)[None, :]
    before = jnp.einsum(
        "hrn,nm->hrm", member.astype(jnp.bfloat16), upper.astype(jnp.bfloat16), preferred_element_type=jnp.float32
    ).astype(jnp.int32)
    counts = jnp.sum(member, axis=2, dtype=jnp.int32)
    r8 = jnp.arange(8)
    ends = jnp.sum(jnp.where(r8[None, :, None] >= r8[None, None, :], counts[:, None, :], 0), axis=2, dtype=jnp.int32)
    starts = ends - counts
    pos = jnp.sum(jnp.where(member, before + starts[:, :, None], 0), axis=1, dtype=jnp.int32)
    seats = jnp.arange(SUB, dtype=jnp.int32)
    src = jnp.sum(
        jnp.where(pos[:, None, :] == seats[None, :, None], seats[None, None, :], 0), axis=2, dtype=jnp.int32
    )
    cut = jnp.minimum(ends[:, :7] // T, NT - 1)
    turn = jnp.arange(7, dtype=jnp.int32)[None, :] + cut
    steps = jnp.arange(NP, dtype=jnp.int32)
    irrep = jnp.sum((turn[:, None, :] < steps[None, :, None]).astype(jnp.int32), axis=2, dtype=jnp.int32)
    tile = steps[None, :] - irrep
    pick = irrep[:, :, None] == r8[None, None, :]
    first = jnp.sum(jnp.where(pick, starts[:, None, :], 0), axis=2, dtype=jnp.int32)
    last = jnp.sum(jnp.where(pick, ends[:, None, :], 0), axis=2, dtype=jnp.int32)
    t4 = jnp.arange(NT, dtype=jnp.int32)
    done = t4[None, :] + jnp.sum((cut[:, None, :] <= t4[None, :, None]).astype(jnp.int32), axis=2, dtype=jnp.int32)
    done = jnp.where(t4[None, :] == NT - 1, NP - 1, done)
    rows = jnp.stack([tile, irrep, first, last], axis=2).reshape(NH, NP * 4)
    tab = jnp.concatenate(
        [rows, jnp.zeros((NH, 48 - NP * 4), jnp.int32), done, jnp.zeros((NH, STRIDE - 48 - NT), jnp.int32)], axis=1
    ).reshape(NH * STRIDE)
    seg = jnp.zeros((NH, 2, 128), jnp.int32).at[:, 0, :8].set(starts).at[:, 1, :8].set(ends)
    return tab, src.reshape(NH, 1, SUB), pos.reshape(NH, 1, SUB), seg


def fused(amplitudes, integrals, occ_irrep, virt_count, c_irrep, a_irrep):
    k_local = amplitudes.shape[1]
    q_local = integrals.shape[2]
    k_first = (lax.axis_index("oo") * lax.axis_size("rep") + lax.axis_index("rep")) * k_local
    q_first = lax.axis_index("vv") * q_local
    k_valid = slot_valid(k_first + jnp.arange(k_local, dtype=jnp.int32), c_irrep, virt_count)
    q_valid = slot_valid(q_first + jnp.arange(q_local, dtype=jnp.int32), a_irrep, virt_count)
    row_irrep = jnp.bitwise_xor(occ_irrep[:, None], occ_irrep[None, :]).reshape(-1)
    tab, src, pos, seg = layout_tables(row_irrep)
    kval = jnp.pad(k_valid.astype(jnp.bfloat16), ((0, 120), (0, 0)))
    qval = q_valid.astype(jnp.float32).reshape(8, q_local // QC, 1, QC)
    vmem = pl.BlockSpec(memory_space=pltpu.VMEM)
    hbm = pl.BlockSpec(memory_space=pl.ANY)
    dma = pltpu.SemaphoreType.DMA
    bf16 = jnp.bfloat16
    return pl.pallas_call(
        ladder_kernel,
        out_shape=jax.ShapeDtypeStruct((SUB, q_local), bf16),
        in_specs=[pl.BlockSpec(memory_space=pltpu.SMEM)] + [vmem] * 5 + [hbm] * 2,
        out_specs=hbm,
        scratch_shapes=[
            pltpu.VMEM((8, NQ, k_local, QC), bf16),
            pltpu.VMEM((NH, SUB, k_local), bf16),
            pltpu.VMEM((NT, T, k_local), bf16),
            pltpu.VMEM((NP + 1, T, QC), bf16),
            pltpu.VMEM((SUB, QC), bf16),
            pltpu.VMEM((2, SUB, QC), bf16),
            pltpu.VMEM((2 * NQ, SUB, QC), bf16),
            pltpu.VMEM((NQ, SUB, QC), bf16),
            dma((8, NQ)), dma((NT,)), dma((NH, 2)), dma((10,)),
            dma((2,)), dma((2 * NQ,)), dma((NQ,)), dma((NQ,)), dma((NQ,)),
        ],
        compiler_params=pltpu.CompilerParams(
            collective_id=0, has_side_effects=True, vmem_limit_bytes=64 * 1024 * 1024 - 256 * 1024
        ),
        cost_estimate=pl.CostEstimate(
            flops=2 * NH * NP * T * k_local * q_local, bytes_accessed=40 * 1024 * 1024, transcendentals=0
        ),
    )(tab, src, pos, seg, kval, qval, amplitudes, integrals)


def solution(mesh):
    placed = (
        P(("grp", "vv"), ("oo", "rep")),
        P(None, ("oo", "rep"), ("grp", "vv")),
        P(),
        P(),
        P(),
        P(),
    )
    shape = dict(mesh.shape)
    same = (shape['vv'], shape['oo'], shape['rep'], shape['grp']) == (4, 2, 2, 2)
    return jax.shard_map(
        fused if same else local,
        mesh=mesh,
        in_specs=placed,
        out_specs=P(("oo", "rep"), ("grp", "vv")),
        check_vma=False,
    )
```
